32 devices in a mesh: ens: 2 (over y), bx: 8 (over z, x), by: 2 (over core).
Axes of the slice: x: 2, y: 2, z: 4, core: 2. Of those that a mesh axis runs over, the one named last changes fastest.
Arguments:
- nodes: bfloat16 [4096, 512], P(('ens', 'bx', 'by')), parts along dimension 0, may hold values from -6 to 6
- edges: bfloat16 [49152, 512], P(('ens', 'bx', 'by')), parts along dimension 0, may hold values from -6 to 6
- edge_cotangent: bfloat16 [49152, 512], P(('ens', 'bx', 'by')), parts along dimension 0, may hold values from -6 to 6
- node_cotangent: bfloat16 [4096, 512], P(('ens', 'bx', 'by')), parts along dimension 0, may hold values from -6 to 6
- senders: int32 [49152], P(('ens', 'bx', 'by')), parts along dimension 0, may hold values from 0 to 127, as said below
- receivers: int32 [49152], P(('ens', 'bx', 'by')), parts along dimension 0, may hold values from 0 to 127
- slots: int32 [384], P(('ens', 'bx', 'by')), parts along dimension 0, may hold values from 0 to 5, as said below
- live: int32 [384], P(('ens', 'bx', 'by')), parts along dimension 0, may hold values from 32 to 128, as said below
- w_edge: bfloat16 [512, 512], P('bx'), may hold values from -0.15625 to 0.15625
- w_send: bfloat16 [512, 512], P('bx'), may hold values from -0.15625 to 0.15625
- w_recv: bfloat16 [512, 512], P('bx'), may hold values from -0.15625 to 0.15625
- w_out: bfloat16 [512, 512], P('bx'), may hold values from -0.25 to 0.25
- bias: float32 [512], replicated, may hold values from -3 to 3
Outputs:
- grad_edges: bfloat16 [49152, 512], P(('ens', 'bx', 'by')), parts along dimension 0
- grad_nodes: bfloat16 [4096, 512], P(('ens', 'bx', 'by')), parts along dimension 0
The draws below stay inside these ranges and needn't reach their ends.
There are 2 independent parts, one for each index of `ens`. The reference program is written for one: setup_inputs(seed, part) draws one part's arguments, and reference() takes and returns one part's arrays. A program takes and returns all parts, laid end to end along the dimension named above; an argument that names none is the same for every part. Nothing has to cross between parts.
Inputs may be any that keep to these rules, and one draw needn't show every extreme that they name: `senders`: in a block of source s, every row's sender (padded rows too) is below 128 for s = 0, below 32 for s = 1, 2, 3 and below 16 for s = 4, 5. `slots`: of the 12 blocks of each patch, exactly two take each of the sources 0 to 5. `live`: the blocks of source 0 of every patch are full.
All inputs are finite; a program needn't handle non-finite values.
Results may differ from the reference program's by a relative error of at most 0.0055.
Values may be sent and summed in bfloat16 or wider, within the bound.
A program may use at most 64 MiB of HBM per device.

```python
import jax
import jax.numpy as jnp
from jax import lax

D = 512
BLOCK = 128
BLK_DEV = 12
NODE_DEV = 128
COARSE = 16
RIM = 32
NODES = 2048
BLOCKS = 192
EDGES = 24576
N_BX = 8
N_BY = 2


def slot_table(key):
    device_keys = jax.random.split(key, N_BX * N_BY)
    table = jax.vmap(lambda dev_key: jax.random.permutation(dev_key, BLK_DEV))(device_keys)
    return (table.reshape(-1) % 6).astype(jnp.int32)


def draw_slots(key, part):
    table = slot_table(key)
    return table


def draw_senders(key, part):
    table = slot_table(key)
    key = jax.random.fold_in(key, 12)
    positions = jnp.arange(EDGES, dtype=jnp.int32)
    edge_slot = jnp.repeat(table, BLOCK)
    extents = jnp.array([NODE_DEV, RIM, RIM, RIM, COARSE, COARSE], dtype=jnp.int32)
    extent = extents[edge_slot]
    raw_draw = jax.random.randint(key, (EDGES,), 0, 1 << 20, dtype=jnp.int32)
    chosen = raw_draw % extent
    in_block = positions % BLOCK
    chosen = jnp.where((edge_slot == 0) & (in_block == 0), NODE_DEV - 1, chosen)
    chosen = jnp.where((edge_slot == 0) & (in_block == 1), 0, chosen)
    return chosen.astype(jnp.int32)


def draw_live(key, part):
    table = slot_table(key)
    key = jax.random.fold_in(key, 13)
    random_live = jax.random.randint(key, (BLOCKS,), BLOCK // 4, BLOCK + 1, dtype=jnp.int32)
    device_of = jnp.arange(BLOCKS, dtype=jnp.int32) // BLK_DEV
    result = jnp.where((table == 1) & (device_of == 0), BLOCK // 4, random_live)
    result = jnp.where(table == 0, BLOCK, result)
    return result.astype(jnp.int32)


def plant(drawn, key, low, top_value):
    longest = drawn.shape.index(max(drawn.shape))
    spots = []
    for shift in (0, 1):
        where = [jax.random.randint(jax.random.fold_in(key, axis), (), 0, length) for axis, length in enumerate(drawn.shape)]
        where[longest] = (where[longest] + shift) % drawn.shape[longest]
        spots.append(tuple(where))
    return drawn.at[spots[0]].set(low).at[spots[1]].set(top_value)


def steps_of(stream_key, dims, shards, smallest, high):
    loudness = 1.0
    for dim, blocks in shards:
        heights = jax.random.uniform(jax.random.fold_in(jax.random.fold_in(stream_key, 6), dim), (blocks,), jnp.float32, smallest / len(shards), high / len(shards))
        loudness = loudness * jnp.repeat(jnp.exp(heights), dims[dim] // blocks).reshape((-1,) + (1,) * (len(dims) - 1 - dim))
    return loudness


def gaussian(rng, shape, deviation, bound, cuts=(), kind=jnp.bfloat16):
    entries = deviation * jax.random.normal(rng, shape, jnp.float32)
    if cuts:
        entries = entries * steps_of(rng, shape, cuts, -0.22, 0.18)
    return jnp.clip(entries, -bound, bound).astype(kind)


def setup_inputs(seed: int = 0, part: int = 0) -> dict:
    key_list = jax.random.split(jax.random.key(seed), 14)
    part_splits = jax.random.split(jax.random.fold_in(key_list[13], part), 14)
    return {
        "nodes": gaussian(part_splits[0], (NODES, D), 1.0, 6.0, ((0, 16),)),
        "edges": gaussian(part_splits[1], (EDGES, D), 1.0, 6.0, ((0, 16),)),
        "edge_cotangent": gaussian(part_splits[2], (EDGES, D), 1.0, 6.0, ((0, 16),)),
        "node_cotangent": gaussian(part_splits[3], (NODES, D), 1.0, 6.0, ((0, 16),)),
        "senders": draw_senders(jax.random.fold_in(jax.random.fold_in(key_list[13], part), 71), part),
        "receivers": plant(jax.random.randint(part_splits[5], (EDGES,), 0, NODE_DEV), jax.random.fold_in(part_splits[5], 1), 0, NODE_DEV - 1).astype(jnp.int32),
        "slots": draw_slots(jax.random.fold_in(jax.random.fold_in(key_list[13], part), 71), part),
        "live": draw_live(jax.random.fold_in(jax.random.fold_in(key_list[13], part), 71), part),
        "w_edge": gaussian(key_list[8], (D, D), (3 * D) ** -0.5, 0.15625, ((0, 8),)),
        "w_send": gaussian(key_list[9], (D, D), (3 * D) ** -0.5, 0.15625, ((0, 8),)),
        "w_recv": gaussian(key_list[10], (D, D), (3 * D) ** -0.5, 0.15625, ((0, 8),)),
        "w_out": gaussian(key_list[11], (D, D), D ** -0.5, 0.25, ((0, 8),)),
        "bias": gaussian(key_list[12], (D,), 0.5, 3.0, (), jnp.float32),
    }


def silu_slope(pre_act):
    sigma = jax.nn.sigmoid(pre_act)
    return sigma * (1.0 + pre_act * (1.0 - sigma))


def reference(nodes, edges, edge_cotangent, node_cotangent, senders, receivers, slots, live, w_edge, w_send, w_recv, w_out, bias):
    patches = N_BX * N_BY
    edge_rows = BLK_DEV * BLOCK
    positions = jnp.arange(EDGES, dtype=jnp.int32)
    block_of = positions // BLOCK
    edge_slot = slots[block_of]
    patch_of = positions // edge_rows
    column_bx = patch_of // N_BY
    column_by = patch_of % N_BY
    source_bx = jnp.where(edge_slot == 1, (column_bx - 1) % N_BX, column_bx)
    source_bx = jnp.where(edge_slot == 2, (column_bx + 1) % N_BX, source_bx)
    source_bx = jnp.where(edge_slot == 4, jnp.bitwise_xor(column_bx, N_BX // 2), source_bx)
    source_bx = jnp.where(edge_slot == 5, jnp.bitwise_xor(column_bx, N_BX // 4), source_bx)
    source_by = jnp.where(edge_slot == 3, 1 - column_by, column_by)
    offsets = jnp.array([0, NODE_DEV - RIM, 0, RIM, 0, 0], dtype=jnp.int32)
    send_node = ((source_bx * N_BY + source_by) * NODE_DEV + offsets[edge_slot] + senders).astype(jnp.int32)
    recv_node = (patch_of * NODE_DEV + receivers).astype(jnp.int32)
    live_mask = ((positions % BLOCK) < live[block_of]).astype(jnp.float32)
    proj_send = jnp.dot(nodes, w_send, preferred_element_type=jnp.float32)
    proj_recv = jnp.dot(nodes, w_recv, preferred_element_type=jnp.float32)

    def per_patch(pieces):
        edge_part, cot_part, send_part, recv_part, mask_part = pieces
        pre_act = jnp.dot(edge_part, w_edge, preferred_element_type=jnp.float32)
        pre_act = pre_act + proj_send[send_part] + proj_recv[recv_part] + bias
        grad_msg = ((cot_part.astype(jnp.float32) + node_cotangent[recv_part].astype(jnp.float32)) * mask_part[:, None]).astype(jnp.bfloat16)
        grad_act = jnp.dot(grad_msg, w_out.T, preferred_element_type=jnp.float32)
        grad_pre = (grad_act * silu_slope(pre_act)).astype(jnp.bfloat16)
        grad_edge = (cot_part.astype(jnp.float32) + jnp.dot(grad_pre, w_edge.T, preferred_element_type=jnp.float32)).astype(jnp.bfloat16)
        return grad_pre, grad_edge

    grad_pre, grad_edges = lax.map(per_patch, (
        edges.reshape(patches, edge_rows, D),
        edge_cotangent.reshape(patches, edge_rows, D),
        send_node.reshape(patches, edge_rows),
        recv_node.reshape(patches, edge_rows),
        live_mask.reshape(patches, edge_rows)))
    grad_pre = grad_pre.reshape(EDGES, D).astype(jnp.float32)
    send_sums = jax.ops.segment_sum(grad_pre, send_node, num_segments=NODES)
    recv_sums = jax.ops.segment_sum(grad_pre, recv_node, num_segments=NODES)
    grad_nodes = node_cotangent.astype(jnp.float32)
    grad_nodes = grad_nodes + jnp.dot(send_sums.astype(jnp.bfloat16), w_send.T, preferred_element_type=jnp.float32)
    grad_nodes = grad_nodes + jnp.dot(recv_sums.astype(jnp.bfloat16), w_recv.T, preferred_element_type=jnp.float32)
    return grad_edges.reshape(EDGES, D), grad_nodes.astype(jnp.bfloat16)
```

```python
import functools

import jax
import jax.numpy as jnp
from jax import lax
from jax.experimental import pallas as pl
from jax.experimental.pallas import tpu as pltpu
from jax.sharding import PartitionSpec as P

COARSE = 16
MESH = pl.DeviceIdType.MESH
NN = (((1,), (0,)), ((), ()))
NT = (((1,), (1,)), ((), ()))


def dot(a, b, dims=NN):
    return lax.dot_general(a, b, dims, preferred_element_type=jnp.float32)


def flip(index, apart):
    return index + apart * (1 - 2 * ((index // apart) % 2))


def kernel(
    cfg,
    slots_ref,
    live_ref,
    senders_ref,
    receivers_ref,
    bias_ref,
    nodes_hbm,
    edges_hbm,
    cot_hbm,
    ncot_hbm,
    wout_hbm,
    wedge_hbm,
    wsend_hbm,
    wrecv_hbm,
    gedges_hbm,
    gnodes_ref,
    wall,
    table,
    edges_v,
    cot_v,
    ncot_v,
    oh,
    oht,
    gmsg,
    gact,
    pre,
    proj,
    gpre,
    sums,
    back_out,
    back_in,
    out_v,
    local_sem,
    out_sem,
    send_sem,
    recv_sem,
):
    n_bx, gather, nz, shard_rows, chunk = cfg
    node_dev = ncot_v.shape[0]
    rim = node_dev // 4
    block = senders_ref.shape[1]
    blocks = senders_ref.shape[0]
    rows = edges_v.shape[0]
    ens, bx, by = lax.axis_index("ens"), lax.axis_index("bx"), lax.axis_index("by")
    z, x = bx // 2, bx % 2

    def local(source, target, number):
        return pltpu.make_async_copy(source, target, local_sem.at[number])

    weights = (wout_hbm, wedge_hbm, wsend_hbm, wrecv_hbm)
    w_copies = []
    for number, ref in enumerate(weights):
        target = wall.at[number, z, x] if gather else wall.at[number]
        w_copies.append(local(ref, target, number))
    nodes_copy = local(nodes_hbm, table.at[pl.ds(0, node_dev)], 4)
    ncot_copy = local(ncot_hbm, ncot_v, 5)
    cot_copy = local(cot_hbm, cot_v, 6)
    edges_copy = local(edges_hbm, edges_v, 7)
    for copy in [nodes_copy] + w_copies + [ncot_copy, cot_copy, edges_copy]:
        copy.start()

    right = (ens, (bx + 1) % n_bx, by)
    left = (ens, (bx + n_bx - 1) % n_bx, by)
    core = (ens, bx, 1 - by)
    far = [(ens, flip(bx, n_bx // 2), by), (ens, flip(bx, n_bx // 4), by)]
    x_peer = (ens, z * 2 + 1 - x, by)
    y_peer = (1 - ens, bx, by)
    greeted = [right, left, core] + far
    if gather:
        greeted += [(ens, ((z + dz) % nz) * 2 + x, by) for dz in range(1, nz)]
        greeted += [x_peer, y_peer]

    barrier = pltpu.get_barrier_semaphore()
    for device in greeted:
        pl.semaphore_signal(barrier, inc=1, device_id=device, device_id_type=MESH)
    pl.semaphore_wait(barrier, len(greeted))

    used = [0]
    sent = []

    def message(source, target, device, incoming):
        number = used[0]
        used[0] += 1
        out = pltpu.make_async_remote_copy(
            src_ref=source,
            dst_ref=target,
            send_sem=send_sem.at[number],
            recv_sem=recv_sem.at[number],
            device_id=device,
            device_id_type=MESH,
        )
        out.start()
        sent.append(out)
        return pltpu.make_async_remote_copy(
            src_ref=incoming,
            dst_ref=incoming,
            send_sem=send_sem.at[number],
            recv_sem=recv_sem.at[number],
            device_id=device,
            device_id_type=MESH,
        )

    nodes_copy.wait()
    pieces = [
        (node_dev - rim, rim, right),
        (0, rim, left),
        (rim, rim, core),
        (0, COARSE, far[0]),
        (0, COARSE, far[1]),
    ]
    node_msgs = []
    place = node_dev
    for start, size, device in pieces:
        target = table.at[pl.ds(place, size)]
        node_msgs.append(message(table.at[pl.ds(start, size)], target, device, target))
        place += size

    def part_a(zz, xx, e, b):
        size = shard_rows // 4
        start = pl.multiple_of((2 * e + b) * size, size)
        return wall.at[pl.ds(0, 2), zz, xx, pl.ds(start, size)]

    def part_b(zz, xx, e, b):
        size = shard_rows // 2
        start = pl.multiple_of(b * size, size)
        return wall.at[pl.ds(2, 2), zz, xx, pl.ds(start, size)]

    def z_sends(part):
        got = []
        own = part(z, x, ens, by)
        for dz in range(1, nz):
            incoming = part((z - dz + nz) % nz, x, ens, by)
            got.append(message(own, own, (ens, ((z + dz) % nz) * 2 + x, by), incoming))
        return got

    def forward(part, dz, xx, e, b, device, arrives):
        zz = (z - dz + nz) % nz
        source = part(zz, xx, e, b)
        return message(source, source, device, part(zz, *arrives))

    def to_x(part, dz):
        return forward(part, dz, x, ens, by, x_peer, (1 - x, ens, by))

    def to_y(part, dz, xx):
        return forward(part, dz, xx, ens, by, y_peer, (xx, 1 - ens, by))

    def to_core(part, dz, xx, e):
        return forward(part, dz, xx, e, by, core, (xx, e, 1 - by))

    def prepare(first, last):
        @pl.loop(first, last)
        def _(number):
            row = pl.multiple_of(number * block, block)
            here = pl.ds(row, block)
            slot = slots_ref[number]
            offset = jnp.where(slot == 0, 0, node_dev)
            offset = offset + jnp.where(slot == 2, rim, 0)
            offset = offset + jnp.where(slot == 3, 2 * rim, 0)
            offset = offset + jnp.where(slot >= 4, 3 * rim, 0)
            offset = offset + jnp.where(slot == 5, COARSE, 0)
            sender = senders_ref[pl.ds(number, 1), :] + offset
            receiver = receivers_ref[pl.ds(number, 1), :]
            lines = lax.broadcasted_iota(jnp.int32, (2 * node_dev, block), 0)
            hot_s = jnp.where(lines == sender, 1.0, 0.0)
            lines = lax.broadcasted_iota(jnp.int32, (node_dev, block), 0)
            hot_r = jnp.where(lines == receiver, 1.0, 0.0)
            hot = jnp.concatenate([hot_s, hot_r], axis=0)
            oht[:, here] = hot.astype(jnp.bfloat16)
            turned = hot.T.astype(jnp.bfloat16)
            oh[here, :] = turned
            ncot = dot(turned[:, 2 * node_dev :], ncot_v[...])
            total = cot_v[here, :].astype(jnp.float32) + ncot
            lines = lax.broadcasted_iota(jnp.int32, total.shape, 0)
            total = jnp.where(lines < live_ref[number], total, 0.0)
            gmsg[here, :] = total.astype(jnp.bfloat16)

    third = blocks // 3
    for copy in w_copies:
        copy.wait()
    if gather:
        a_z = z_sends(part_a)
        a_x = [to_x(part_a, 0)]
        b_z = z_sends(part_b)
        b_x = [to_x(part_b, 0)]
    ncot_copy.wait()
    cot_copy.wait()
    prepare(0, third)
    a_y, a_c, a_c2, b_c = [], [], [], []
    if gather:
        for dz in range(1, nz):
            a_z[dz - 1].wait_recv()
            a_x.append(to_x(part_a, dz))
            a_y.append((dz, x, to_y(part_a, dz, x)))
            a_c.append(to_core(part_a, dz, x, ens))
        prepare(third, 2 * third)
        for dz in range(nz):
            a_x[dz].wait_recv()
            a_y.append((dz, 1 - x, to_y(part_a, dz, 1 - x)))
            a_c.append(to_core(part_a, dz, 1 - x, ens))
        for dz in range(1, nz):
            b_z[dz - 1].wait_recv()
            b_x.append(to_x(part_b, dz))
            b_c.append(to_core(part_b, dz, x, ens))
        prepare(2 * third, blocks)
        for dz, xx, arrival in a_y:
            arrival.wait_recv()
            a_c2.append(to_core(part_a, dz, xx, 1 - ens))
        for dz in range(nz):
            b_x[dz].wait_recv()
            b_c.append(to_core(part_b, dz, 1 - x, ens))
        for arrival in a_c + a_c2:
            arrival.wait_recv()
    else:
        prepare(third, blocks)

    def weight(number):
        value = wall[number]
        return value.reshape(-1, value.shape[-1])

    edges_copy.wait()

    @pl.loop(0, rows // chunk)
    def _(number):
        here = pl.ds(pl.multiple_of(number * chunk, chunk), chunk)
        gact[here, :] = dot(gmsg[here, :], weight(0), NT)
        pre[here, :] = dot(edges_v[here, :], weight(1)) + bias_ref[...]

    for arrival in b_c + node_msgs:
        arrival.wait_recv()
    proj[pl.ds(0, 2 * node_dev), :] = dot(table[...], weight(2)).astype(jnp.bfloat16)
    proj[pl.ds(2 * node_dev, node_dev), :] = dot(
        table[pl.ds(0, node_dev), :], weight(3)
    ).astype(jnp.bfloat16)

    @pl.loop(0, rows // chunk)
    def _(number):
        here = pl.ds(pl.multiple_of(number * chunk, chunk), chunk)
        act = pre[here, :] + dot(oh[here, :], proj[...])
        sigma = 0.5 + 0.5 * jnp.tanh(0.5 * act)
        slope = sigma * (1.0 + act * (1.0 - sigma))
        gpre[here, :] = (gact[here, :] * slope).astype(jnp.bfloat16)

    sums[...] = dot(oht[...], gpre[...])
    back_out[...] = sums[pl.ds(node_dev, node_dev), :].astype(jnp.bfloat16)
    backs = [(rim, left), (rim, right), (rim, core), (COARSE, far[0]), (COARSE, far[1])]
    back_msgs = []
    place = 0
    for size, device in backs:
        here = pl.ds(place, size)
        back_msgs.append(message(back_out.at[here], back_in.at[here], device, back_in.at[here]))
        place += size

    outs = []
    for number in range(rows // chunk):
        here = pl.ds(number * chunk, chunk)
        out_v[here, :] = (
            cot_v[here, :].astype(jnp.float32) + dot(gpre[here, :], weight(1), NT)
        ).astype(jnp.bfloat16)
        copy = pltpu.make_async_copy(out_v.at[here], gedges_hbm.at[here], out_sem.at[number])
        copy.start()
        outs.append(copy)

    received = dot(
        sums[pl.ds(2 * node_dev, node_dev), :].astype(jnp.bfloat16), weight(3), NT
    ) + ncot_v[...].astype(jnp.float32)
    for arrival in back_msgs:
        arrival.wait_recv()
    own = sums[pl.ds(0, node_dev), :]
    got = back_in[...].astype(jnp.float32)
    coarse = got[3 * rim : 3 * rim + COARSE] + got[3 * rim + COARSE :]
    low = own[:rim] + got[rim : 2 * rim]
    low = jnp.concatenate([low[:COARSE] + coarse, low[COARSE:]], axis=0)
    middle = own[rim : 2 * rim] + got[2 * rim : 3 * rim]
    high = own[node_dev - rim :] + got[:rim]
    own = jnp.concatenate([low, middle, own[2 * rim : node_dev - rim], high], axis=0)
    gnodes_ref[...] = (received + dot(own.astype(jnp.bfloat16), weight(2), NT)).astype(
        jnp.bfloat16
    )
    for copy in sent:
        copy.wait_send()
    for copy in outs:
        copy.wait()


def per_device(
    n_bx,
    nodes,
    edges,
    edge_cotangent,
    node_cotangent,
    senders,
    receivers,
    slots,
    live,
    w_edge,
    w_send,
    w_recv,
    w_out,
    bias,
):
    shard_rows, width = w_edge.shape
    depth = shard_rows * n_bx
    gather = shard_rows % 64 == 0 and n_bx % 2 == 0
    weights = [w_out, w_edge, w_send, w_recv]
    if not gather:
        weights = [lax.all_gather(w, "bx", axis=0, tiled=True) for w in weights]
    nz = n_bx // 2
    rows = edges.shape[0]
    blocks = slots.shape[0]
    block = rows // blocks
    node_dev = nodes.shape[0]
    chunk = rows // 3
    cfg = (n_bx, gather, nz, shard_rows, chunk)
    bf16, f32 = jnp.bfloat16, jnp.float32
    wall = (4, nz, 2, shard_rows, width) if gather else (4, depth, width)
    count = 3 * nz + 64
    smem = pl.BlockSpec(memory_space=pltpu.SMEM)
    vmem = pl.BlockSpec(memory_space=pltpu.VMEM)
    hbm = pl.BlockSpec(memory_space=pl.ANY)
    return pl.pallas_call(
        functools.partial(kernel, cfg),
        out_shape=(
            jax.ShapeDtypeStruct((rows, width), bf16),
            jax.ShapeDtypeStruct((node_dev, width), bf16),
        ),
        in_specs=[smem, smem, vmem, vmem, vmem] + [hbm] * 8,
        out_specs=(hbm, vmem),
        scratch_shapes=[
            pltpu.VMEM(wall, bf16),
            pltpu.VMEM((2 * node_dev, width), bf16),
            pltpu.VMEM((rows, width), bf16),
            pltpu.VMEM((rows, width), bf16),
            pltpu.VMEM((node_dev, width), bf16),
            pltpu.VMEM((rows, 3 * node_dev), bf16),
            pltpu.VMEM((3 * node_dev, rows), bf16),
            pltpu.VMEM((rows, width), bf16),
            pltpu.VMEM((rows, width), f32),
            pltpu.VMEM((rows, width), f32),
            pltpu.VMEM((3 * node_dev, width), bf16),
            pltpu.VMEM((rows, width), bf16),
            pltpu.VMEM((3 * node_dev, width), f32),
            pltpu.VMEM((node_dev, width), bf16),
            pltpu.VMEM((node_dev, width), bf16),
            pltpu.VMEM((rows, width), bf16),
            pltpu.SemaphoreType.DMA((8,)),
            pltpu.SemaphoreType.DMA((rows // chunk,)),
            pltpu.SemaphoreType.DMA((count,)),
            pltpu.SemaphoreType.DMA((count,)),
        ],
        compiler_params=pltpu.CompilerParams(
            collective_id=0, has_side_effects=True, vmem_limit_bytes=48 * 1024 * 1024
        ),
    )(
        slots,
        live,
        senders.reshape(blocks, block),
        receivers.reshape(blocks, block),
        bias.reshape(1, width),
        nodes,
        edges,
        edge_cotangent,
        node_cotangent,
        *weights,
    )


def solution(mesh):
    n_bx = mesh.shape["bx"]
    in_specs = (
        P(("ens", "bx", "by"), None),
        P(("ens", "bx", "by"), None),
        P(("ens", "bx", "by"), None),
        P(("ens", "bx", "by"), None),
        P(("ens", "bx", "by")),
        P(("ens", "bx", "by")),
        P(("ens", "bx", "by")),
        P(("ens", "bx", "by")),
        P("bx", None),
        P("bx", None),
        P("bx", None),
        P("bx", None),
        P(),
    )
    out_specs = (P(("ens", "bx", "by"), None), P(("ens", "bx", "by"), None))
    return jax.shard_map(
        functools.partial(per_device, n_bx),
        mesh=mesh,
        in_specs=in_specs,
        out_specs=out_specs,
        check_vma=False,
    )
```

```python
import functools

import jax
import jax.numpy as jnp
from jax import lax
from jax.experimental import pallas as pl
from jax.experimental.pallas import tpu as pltpu
from jax.sharding import PartitionSpec as P

COARSE = 16
MESH = pl.DeviceIdType.MESH
NN = (((1,), (0,)), ((), ()))
NT = (((1,), (1,)), ((), ()))


def dot(a, b, dims=NN):
    return lax.dot_general(a, b, dims, preferred_element_type=jnp.float32)


def flip(index, apart):
    return index + apart * (1 - 2 * ((index // apart) % 2))


def kernel(
    cfg,
    slots_hbm,
    live_hbm,
    senders_hbm,
    receivers_hbm,
    bias_hbm,
    nodes_hbm,
    edges_hbm,
    cot_hbm,
    ncot_hbm,
    wout_hbm,
    wedge_hbm,
    wsend_hbm,
    wrecv_hbm,
    gedges_ref,
    gnodes_ref,
    slots_ref,
    live_ref,
    senders_ref,
    receivers_ref,
    bias_ref,
    wall,
    table,
    edges_v,
    cot_v,
    ncot_v,
    oh,
    oht,
    gmsg,
    gact,
    pre,
    proj,
    gpre,
    back_out,
    back_in,
    local_sem,
    send_sem,
    recv_sem,
):
    n_bx, gather, nz, shard_rows, chunk = cfg
    node_dev = ncot_v.shape[0]
    rim = node_dev // 4
    block = senders_ref.shape[1]
    blocks = senders_ref.shape[0]
    rows = edges_v.shape[0]
    ens, bx, by = lax.axis_index("ens"), lax.axis_index("bx"), lax.axis_index("by")
    z, x = bx // 2, bx % 2

    def local(source, target, number):
        return pltpu.make_async_copy(source, target, local_sem.at[number])

    weights = (wout_hbm, wedge_hbm, wsend_hbm, wrecv_hbm)
    w_copies = []
    for number, ref in enumerate(weights):
        target = wall.at[number, z, x] if gather else wall.at[number]
        w_copies.append(local(ref, target, number))
    nodes_copy = local(nodes_hbm, table.at[pl.ds(0, node_dev)], 4)
    ncot_copy = local(ncot_hbm, ncot_v, 5)
    cot_copy = local(cot_hbm, cot_v, 6)
    edges_copy = local(edges_hbm, edges_v, 7)
    small_copies = [
        local(slots_hbm, slots_ref, 8),
        local(live_hbm, live_ref, 9),
        local(senders_hbm, senders_ref, 10),
        local(receivers_hbm, receivers_ref, 11),
        local(bias_hbm, bias_ref, 12),
    ]
    for copy in [nodes_copy] + w_copies + small_copies + [ncot_copy, cot_copy, edges_copy]:
        copy.start()

    right = (ens, (bx + 1) % n_bx, by)
    left = (ens, (bx + n_bx - 1) % n_bx, by)
    core = (ens, bx, 1 - by)
    far = [(ens, flip(bx, n_bx // 2), by), (ens, flip(bx, n_bx // 4), by)]
    x_peer = (ens, z * 2 + 1 - x, by)
    y_peer = (1 - ens, bx, by)
    greeted = [right, left, core] + far
    if gather:
        greeted += [(ens, ((z + dz) % nz) * 2 + x, by) for dz in range(1, nz)]
        greeted += [x_peer, y_peer]

    barrier = pltpu.get_barrier_semaphore()
    for device in greeted:
        pl.semaphore_signal(barrier, inc=1, device_id=device, device_id_type=MESH)
    pl.semaphore_wait(barrier, len(greeted))

    used = [0]
    sent = []

    def message(source, target, device, incoming):
        number = used[0]
        used[0] += 1
        out = pltpu.make_async_remote_copy(
            src_ref=source,
            dst_ref=target,
            send_sem=send_sem.at[number],
            recv_sem=recv_sem.at[number],
            device_id=device,
            device_id_type=MESH,
        )
        out.start()
        sent.append(out)
        return pltpu.make_async_remote_copy(
            src_ref=incoming,
            dst_ref=incoming,
            send_sem=send_sem.at[number],
            recv_sem=recv_sem.at[number],
            device_id=device,
            device_id_type=MESH,
        )

    nodes_copy.wait()
    pieces = [
        (node_dev - rim, rim, right),
        (0, rim, left),
        (rim, rim, core),
        (0, COARSE, far[0]),
        (0, COARSE, far[1]),
    ]
    node_msgs = []
    place = node_dev
    for start, size, device in pieces:
        target = table.at[pl.ds(place, size)]
        node_msgs.append(message(table.at[pl.ds(start, size)], target, device, target))
        place += size

    def part_a(zz, xx, e, b):
        size = shard_rows // 4
        start = pl.multiple_of((2 * e + b) * size, size)
        return wall.at[pl.ds(0, 2), zz, xx, pl.ds(start, size)]

    def part_b(zz, xx, e, b):
        size = shard_rows // 2
        start = pl.multiple_of(b * size, size)
        return wall.at[pl.ds(2, 2), zz, xx, pl.ds(start, size)]

    def z_sends(part):
        got = []
        own = part(z, x, ens, by)
        for dz in range(1, nz):
            incoming = part((z - dz + nz) % nz, x, ens, by)
            got.append(message(own, own, (ens, ((z + dz) % nz) * 2 + x, by), incoming))
        return got

    def forward(part, dz, xx, e, b, device, arrives):
        zz = (z - dz + nz) % nz
        source = part(zz, xx, e, b)
        return message(source, source, device, part(zz, *arrives))

    def to_x(part, dz):
        return forward(part, dz, x, ens, by, x_peer, (1 - x, ens, by))

    def to_y(part, dz, xx):
        return forward(part, dz, xx, ens, by, y_peer, (xx, 1 - ens, by))

    def to_core(part, dz, xx, e):
        return forward(part, dz, xx, e, by, core, (xx, e, 1 - by))

    def prepare(first, last):
        @pl.loop(first, last)
        def _(number):
            row = pl.multiple_of(number * block, block)
            here = pl.ds(row, block)
            slot = slots_ref[number]
            offset = jnp.where(slot == 0, 0, node_dev)
            offset = offset + jnp.where(slot == 2, rim, 0)
            offset = offset + jnp.where(slot == 3, 2 * rim, 0)
            offset = offset + jnp.where(slot >= 4, 3 * rim, 0)
            offset = offset + jnp.where(slot == 5, COARSE, 0)
            sender = senders_ref[pl.ds(number, 1), :] + offset
            receiver = receivers_ref[pl.ds(number, 1), :]
            lines = lax.broadcasted_iota(jnp.int32, (2 * node_dev, block), 0)
            hot_s = jnp.where(lines == sender, 1.0, 0.0)
            lines = lax.broadcasted_iota(jnp.int32, (node_dev, block), 0)
            hot_r = jnp.where(lines == receiver, 1.0, 0.0)
            hot = jnp.concatenate([hot_s, hot_r], axis=0)
            oht[:, here] = hot.astype(jnp.bfloat16)
            turned = hot.T.astype(jnp.bfloat16)
            oh[here, :] = turned
            ncot = dot(turned[:, 2 * node_dev :], ncot_v[...])
            total = cot_v[here, :].astype(jnp.float32) + ncot
            lines = lax.broadcasted_iota(jnp.int32, total.shape, 0)
            total = jnp.where(lines < live_ref[number], total, 0.0)
            gmsg[here, :] = total.astype(jnp.bfloat16)

    third = blocks // 3
    for copy in w_copies:
        copy.wait()
    if gather:
        a_z = z_sends(part_a)
        a_x = [to_x(part_a, 0)]
        b_z = z_sends(part_b)
        b_x = [to_x(part_b, 0)]
    for copy in small_copies + [ncot_copy, cot_copy]:
        copy.wait()
    prepare(0, third)
    a_y, a_c, a_c2, b_c = [], [], [], []
    if gather:
        for dz in range(1, nz):
            a_z[dz - 1].wait_recv()
            a_x.append(to_x(part_a, dz))
            a_y.append((dz, x, to_y(part_a, dz, x)))
            a_c.append(to_core(part_a, dz, x, ens))
        prepare(third, 2 * third)
        for dz in range(nz):
            a_x[dz].wait_recv()
            a_y.append((dz, 1 - x, to_y(part_a, dz, 1 - x)))
            a_c.append(to_core(part_a, dz, 1 - x, ens))
        for dz in range(1, nz):
            b_z[dz - 1].wait_recv()
            b_x.append(to_x(part_b, dz))
            b_c.append(to_core(part_b, dz, x, ens))
        prepare(2 * third, blocks)
        for dz, xx, arrival in a_y:
            arrival.wait_recv()
            a_c2.append(to_core(part_a, dz, xx, 1 - ens))
        for dz in range(nz):
            b_x[dz].wait_recv()
            b_c.append(to_core(part_b, dz, 1 - x, ens))
        for arrival in a_c + a_c2:
            arrival.wait_recv()
    else:
        prepare(third, blocks)

    def weight(number):
        value = wall[number]
        return value.reshape(-1, value.shape[-1])

    edges_copy.wait()

    @pl.loop(0, rows // chunk)
    def _(number):
        here = pl.ds(pl.multiple_of(number * chunk, chunk), chunk)
        gact[here, :] = dot(gmsg[here, :], weight(0), NT)
        pre[here, :] = dot(edges_v[here, :], weight(1)) + bias_ref[...]

    for arrival in b_c + node_msgs:
        arrival.wait_recv()
    proj[pl.ds(0, 2 * node_dev), :] = dot(table[...], weight(2)).astype(jnp.bfloat16)
    proj[pl.ds(2 * node_dev, node_dev), :] = dot(
        table[pl.ds(0, node_dev), :], weight(3)
    ).astype(jnp.bfloat16)

    @pl.loop(0, rows // chunk)
    def _(number):
        here = pl.ds(pl.multiple_of(number * chunk, chunk), chunk)
        act = pre[here, :] + dot(oh[here, :], proj[...])
        sigma = 0.5 + 0.5 * jnp.tanh(0.5 * act)
        slope = sigma * (1.0 + act * (1.0 - sigma))
        gpre[here, :] = (gact[here, :] * slope).astype(jnp.bfloat16)

    back_out[...] = dot(oht[pl.ds(node_dev, node_dev), :], gpre[...]).astype(jnp.bfloat16)
    backs = [(rim, left), (rim, right), (rim, core), (COARSE, far[0]), (COARSE, far[1])]
    back_msgs = []
    place = 0
    for size, device in backs:
        here = pl.ds(place, size)
        back_msgs.append(message(back_out.at[here], back_in.at[here], device, back_in.at[here]))
        place += size

    @pl.loop(0, rows // chunk)
    def _(number):
        here = pl.ds(pl.multiple_of(number * chunk, chunk), chunk)
        gedges_ref[here, :] = (
            cot_v[here, :].astype(jnp.float32) + dot(gpre[here, :], weight(1), NT)
        ).astype(jnp.bfloat16)

    own = dot(oht[pl.ds(0, node_dev), :], gpre[...])
    received = dot(oht[pl.ds(2 * node_dev, node_dev), :], gpre[...])
    received = dot(received.astype(jnp.bfloat16), weight(3), NT) + ncot_v[...].astype(
        jnp.float32
    )
    for arrival in back_msgs:
        arrival.wait_recv()
    got = back_in[...].astype(jnp.float32)
    coarse = got[3 * rim : 3 * rim + COARSE] + got[3 * rim + COARSE :]
    low = own[:rim] + got[rim : 2 * rim]
    low = jnp.concatenate([low[:COARSE] + coarse, low[COARSE:]], axis=0)
    middle = own[rim : 2 * rim] + got[2 * rim : 3 * rim]
    high = own[node_dev - rim :] + got[:rim]
    own = jnp.concatenate([low, middle, own[2 * rim : node_dev - rim], high], axis=0)
    gnodes_ref[...] = (received + dot(own.astype(jnp.bfloat16), weight(2), NT)).astype(
        jnp.bfloat16
    )
    for copy in sent:
        copy.wait_send()


def write_out(edges_ref, nodes_ref, edges_hbm, nodes_hbm, sem):
    quarter = edges_ref.shape[0] // 4
    copies = [pltpu.make_async_copy(nodes_ref, nodes_hbm, sem.at[4])]
    for number in range(4):
        here = pl.ds(number * quarter, quarter)
        copies.append(
            pltpu.make_async_copy(edges_ref.at[here], edges_hbm.at[here], sem.at[number])
        )
    for copy in copies:
        copy.start()
    for copy in copies:
        copy.wait()


def per_device(
    n_bx,
    nodes,
    edges,
    edge_cotangent,
    node_cotangent,
    senders,
    receivers,
    slots,
    live,
    w_edge,
    w_send,
    w_recv,
    w_out,
    bias,
):
    shard_rows, width = w_edge.shape
    depth = shard_rows * n_bx
    gather = shard_rows % 64 == 0 and n_bx % 2 == 0
    weights = [w_out, w_edge, w_send, w_recv]
    if not gather:
        weights = [lax.all_gather(w, "bx", axis=0, tiled=True) for w in weights]
    nz = n_bx // 2
    rows = edges.shape[0]
    blocks = slots.shape[0]
    block = rows // blocks
    node_dev = nodes.shape[0]
    chunk = rows // 3
    cfg = (n_bx, gather, nz, shard_rows, chunk)
    bf16, f32 = jnp.bfloat16, jnp.float32
    wall = (4, nz, 2, shard_rows, width) if gather else (4, depth, width)
    count = 3 * nz + 64
    vmem = pl.BlockSpec(memory_space=pltpu.VMEM)
    hbm = pl.BlockSpec(memory_space=pl.ANY)
    results = pl.pallas_call(
        functools.partial(kernel, cfg),
        out_shape=(
            pltpu.VMEM((rows, width), bf16),
            pltpu.VMEM((node_dev, width), bf16),
        ),
        in_specs=[hbm] * 13,
        out_specs=(vmem, vmem),
        scratch_shapes=[
            pltpu.SMEM((blocks,), jnp.int32),
            pltpu.SMEM((blocks,), jnp.int32),
            pltpu.VMEM((blocks, block), jnp.int32),
            pltpu.VMEM((blocks, block), jnp.int32),
            pltpu.VMEM((1, width), f32),
            pltpu.VMEM(wall, bf16),
            pltpu.VMEM((2 * node_dev, width), bf16),
            pltpu.VMEM((rows, width), bf16),
            pltpu.VMEM((rows, width), bf16),
            pltpu.VMEM((node_dev, width), bf16),
            pltpu.VMEM((rows, 3 * node_dev), bf16),
            pltpu.VMEM((3 * node_dev, rows), bf16),
            pltpu.VMEM((rows, width), bf16),
            pltpu.VMEM((rows, width), f32),
            pltpu.VMEM((rows, width), f32),
            pltpu.VMEM((3 * node_dev, width), bf16),
            pltpu.VMEM((rows, width), bf16),
            pltpu.VMEM((node_dev, width), bf16),
            pltpu.VMEM((node_dev, width), bf16),
            pltpu.SemaphoreType.DMA((13,)),
            pltpu.SemaphoreType.DMA((count,)),
            pltpu.SemaphoreType.DMA((count,)),
        ],
        compiler_params=pltpu.CompilerParams(
            collective_id=0, has_side_effects=True, vmem_limit_bytes=60 * 1024 * 1024
        ),
    )(
        slots,
        live,
        senders.reshape(blocks, block),
        receivers.reshape(blocks, block),
        bias.reshape(1, width),
        nodes,
        edges,
        edge_cotangent,
        node_cotangent,
        *weights,
    )
    return pl.pallas_call(
        write_out,
        out_shape=(
            jax.ShapeDtypeStruct((rows, width), bf16),
            jax.ShapeDtypeStruct((node_dev, width), bf16),
        ),
        in_specs=[vmem, vmem],
        out_specs=(hbm, hbm),
        scratch_shapes=[pltpu.SemaphoreType.DMA((5,))],
        compiler_params=pltpu.CompilerParams(vmem_limit_bytes=1024 * 1024),
    )(*results)


def solution(mesh):
    n_bx = mesh.shape["bx"]
    in_specs = (
        P(("ens", "bx", "by"), None),
        P(("ens", "bx", "by"), None),
        P(("ens", "bx", "by"), None),
        P(("ens", "bx", "by"), None),
        P(("ens", "bx", "by")),
        P(("ens", "bx", "by")),
        P(("ens", "bx", "by")),
        P(("ens", "bx", "by")),
        P("bx", None),
        P("bx", None),
        P("bx", None),
        P("bx", None),
        P(),
    )
    out_specs = (P(("ens", "bx", "by"), None), P(("ens", "bx", "by"), None))
    return jax.shard_map(
        functools.partial(per_device, n_bx),
        mesh=mesh,
        in_specs=in_specs,
        out_specs=out_specs,
        check_vma=False,
    )
```

```python
import functools

import jax
import jax.numpy as jnp
from jax import lax
from jax.experimental import pallas as pl
from jax.experimental.pallas import tpu as pltpu
from jax.sharding import PartitionSpec as P

COARSE = 16
MESH = pl.DeviceIdType.MESH
NN = (((1,), (0,)), ((), ()))
NT = (((1,), (1,)), ((), ()))


def dot(a, b, dims=NN):
    return lax.dot_general(a, b, dims, preferred_element_type=jnp.float32)


def flip(index, apart):
    return index + apart * (1 - 2 * ((index // apart) % 2))


def kernel(
    cfg,
    slots_hbm,
    live_hbm,
    senders_hbm,
    receivers_hbm,
    bias_hbm,
    nodes_hbm,
    edges_hbm,
    cot_hbm,
    ncot_hbm,
    wout_hbm,
    wedge_hbm,
    wsend_hbm,
    wrecv_hbm,
    gedges_ref,
    gnodes_ref,
    slots_ref,
    live_ref,
    senders_ref,
    receivers_ref,
    bias_ref,
    wall,
    table,
    edges_v,
    cot_v,
    ncot_v,
    oh,
    oht,
    gmsg,
    gact,
    pre,
    proj,
    gpre,
    back_out,
    back_in,
    local_sem,
    send_sem,
    recv_sem,
):
    n_bx, gather, nz, shard_rows, chunk = cfg
    node_dev = ncot_v.shape[0]
    rim = node_dev // 4
    block = senders_ref.shape[1]
    blocks = senders_ref.shape[0]
    rows = edges_v.shape[0]
    ens, bx, by = lax.axis_index("ens"), lax.axis_index("bx"), lax.axis_index("by")
    z, x = bx // 2, bx % 2

    def local(source, target, number):
        return pltpu.make_async_copy(source, target, local_sem.at[number])

    weights = (wout_hbm, wedge_hbm, wsend_hbm, wrecv_hbm)
    w_copies = []
    for number, ref in enumerate(weights):
        target = wall.at[number, z, x] if gather else wall.at[number]
        w_copies.append(local(ref, target, number))
    nodes_copy = local(nodes_hbm, table.at[pl.ds(0, node_dev)], 4)
    ncot_copy = local(ncot_hbm, ncot_v, 5)
    cot_copy = local(cot_hbm, cot_v, 6)
    edges_copy = local(edges_hbm, edges_v, 7)
    small_copies = [
        local(slots_hbm, slots_ref, 8),
        local(live_hbm, live_ref, 9),
        local(senders_hbm, senders_ref, 10),
        local(receivers_hbm, receivers_ref, 11),
        local(bias_hbm, bias_ref, 12),
    ]
    for copy in [nodes_copy] + w_copies + small_copies + [ncot_copy, cot_copy, edges_copy]:
        copy.start()

    right = (ens, (bx + 1) % n_bx, by)
    left = (ens, (bx + n_bx - 1) % n_bx, by)
    core = (ens, bx, 1 - by)
    far = [(ens, flip(bx, n_bx // 2), by), (ens, flip(bx, n_bx // 4), by)]
    x_peer = (ens, z * 2 + 1 - x, by)
    y_peer = (1 - ens, bx, by)
    greeted = [right, left, core] + far
    if gather:
        greeted += [(ens, ((z + dz) % nz) * 2 + x, by) for dz in range(1, nz)]
        greeted += [x_peer, y_peer]

    barrier = pltpu.get_barrier_semaphore()
    for device in greeted:
        pl.semaphore_signal(barrier, inc=1, device_id=device, device_id_type=MESH)
    pl.semaphore_wait(barrier, len(greeted))

    used = [0]
    sent = []

    def message(source, target, device, incoming):
        number = used[0]
        used[0] += 1
        out = pltpu.make_async_remote_copy(
            src_ref=source,
            dst_ref=target,
            send_sem=send_sem.at[number],
            recv_sem=recv_sem.at[number],
            device_id=device,
            device_id_type=MESH,
        )
        out.start()
        sent.append(out)
        return pltpu.make_async_remote_copy(
            src_ref=incoming,
            dst_ref=incoming,
            send_sem=send_sem.at[number],
            recv_sem=recv_sem.at[number],
            device_id=device,
            device_id_type=MESH,
        )

    nodes_copy.wait()
    pieces = [
        (node_dev - rim, rim, right),
        (0, rim, left),
        (rim, rim, core),
        (0, COARSE, far[0]),
        (0, COARSE, far[1]),
    ]
    shared = 2

    def part_a(zz, xx, e, b):
        size = shard_rows // 4
        start = pl.multiple_of((2 * e + b) * size, size)
        return wall.at[pl.ds(0, shared), zz, xx, pl.ds(start, size)]

    def part_b(zz, xx, e, b):
        size = shard_rows // 2
        start = pl.multiple_of(b * size, size)
        return wall.at[pl.ds(shared, 4 - shared), zz, xx, pl.ds(start, size)]

    def other(step):
        out = z
        if step & 1:
            out = flip(out, 1)
        if step & 2:
            out = flip(out, 2)
        return out

    def z_sends(part):
        got = []
        own = part(z, x, ens, by)
        for dz in range(1, nz):
            incoming = part(other(dz), x, ens, by)
            got.append(message(own, own, (ens, other(dz) * 2 + x, by), incoming))
        return got

    def forward(part, dz, xx, e, b, device, arrives):
        zz = other(dz)
        source = part(zz, xx, e, b)
        return message(source, source, device, part(zz, *arrives))

    def to_x(part, dz):
        return forward(part, dz, x, ens, by, x_peer, (1 - x, ens, by))

    def to_y(part, dz, xx):
        return forward(part, dz, xx, ens, by, y_peer, (xx, 1 - ens, by))

    def to_core(part, dz, xx, e):
        return forward(part, dz, xx, e, by, core, (xx, e, 1 - by))

    def prepare(first, last):
        @pl.loop(first, last)
        def _(number):
            row = pl.multiple_of(number * block, block)
            here = pl.ds(row, block)
            slot = slots_ref[number]
            offset = jnp.where(slot == 0, 0, node_dev)
            offset = offset + jnp.where(slot == 2, rim, 0)
            offset = offset + jnp.where(slot == 3, 2 * rim, 0)
            offset = offset + jnp.where(slot >= 4, 3 * rim, 0)
            offset = offset + jnp.where(slot == 5, COARSE, 0)
            sender = senders_ref[pl.ds(number, 1), :] + offset
            receiver = receivers_ref[pl.ds(number, 1), :]
            lines = lax.broadcasted_iota(jnp.int32, (2 * node_dev, block), 0)
            hot_s = jnp.where(lines == sender, 1.0, 0.0)
            lines = lax.broadcasted_iota(jnp.int32, (node_dev, block), 0)
            hot_r = jnp.where(lines == receiver, 1.0, 0.0)
            hot = jnp.concatenate([hot_s, hot_r], axis=0)
            oht[:, here] = hot.astype(jnp.bfloat16)
            turned = hot.T.astype(jnp.bfloat16)
            oh[here, :] = turned
            ncot = dot(turned[:, 2 * node_dev :], ncot_v[...])
            total = cot_v[here, :].astype(jnp.float32) + ncot
            lines = lax.broadcasted_iota(jnp.int32, total.shape, 0)
            total = jnp.where(lines < live_ref[number], total, 0.0)
            gmsg[here, :] = total.astype(jnp.bfloat16)

    third = blocks // 3
    for copy in w_copies:
        copy.wait()
    if gather:
        a_z = z_sends(part_a)
        a_x = [to_x(part_a, 0)]
    node_msgs = []
    place = node_dev
    for start, size, device in pieces:
        target = table.at[pl.ds(place, size)]
        node_msgs.append(message(table.at[pl.ds(start, size)], target, device, target))
        place += size
    if gather:
        b_z = z_sends(part_b)
        b_x = [to_x(part_b, 0)]
    for copy in small_copies + [ncot_copy, cot_copy]:
        copy.wait()
    prepare(0, third)
    a_y, a_c, a_c2, b_c = [], [], [], []
    if gather:
        for dz in range(1, nz):
            a_z[dz - 1].wait_recv()
            a_x.append(to_x(part_a, dz))
            a_y.append((dz, x, to_y(part_a, dz, x)))
            a_c.append(to_core(part_a, dz, x, ens))
        prepare(third, 2 * third)
        for dz in range(nz):
            a_x[dz].wait_recv()
            a_y.append((dz, 1 - x, to_y(part_a, dz, 1 - x)))
            a_c.append(to_core(part_a, dz, 1 - x, ens))
        for dz in range(1, nz):
            b_z[dz - 1].wait_recv()
            b_x.append(to_x(part_b, dz))
            b_c.append(to_core(part_b, dz, x, ens))
        prepare(2 * third, blocks)
        for dz, xx, arrival in a_y:
            arrival.wait_recv()
            a_c2.append(to_core(part_a, dz, xx, 1 - ens))
        for dz in range(nz):
            b_x[dz].wait_recv()
            b_c.append(to_core(part_b, dz, 1 - x, ens))
        for arrival in a_c + a_c2:
            arrival.wait_recv()
    else:
        prepare(third, blocks)

    def weight(number):
        value = wall[number]
        return value.reshape(-1, value.shape[-1])

    edges_copy.wait()

    for arrival in b_c + node_msgs:
        arrival.wait_recv()
    proj[pl.ds(0, 2 * node_dev), :] = dot(table[...], weight(2)).astype(jnp.bfloat16)
    proj[pl.ds(2 * node_dev, node_dev), :] = dot(
        table[pl.ds(0, node_dev), :], weight(3)
    ).astype(jnp.bfloat16)

    for number in range(rows // chunk):
        here = pl.ds(number * chunk, chunk)
        act = dot(edges_v[here, :], weight(1)) + dot(oh[here, :], proj[...]) + bias_ref[...]
        sigma = 0.5 + 0.5 * jnp.tanh(0.5 * act)
        slope = sigma * (1.0 + act * (1.0 - sigma))
        gpre[here, :] = (dot(gmsg[here, :], weight(0), NT) * slope).astype(jnp.bfloat16)

    back_out[...] = dot(oht[pl.ds(node_dev, node_dev), :], gpre[...]).astype(jnp.bfloat16)
    backs = [(rim, left), (rim, right), (rim, core), (COARSE, far[0]), (COARSE, far[1])]
    back_msgs = []
    place = 0
    for size, device in backs:
        here = pl.ds(place, size)
        back_msgs.append(message(back_out.at[here], back_in.at[here], device, back_in.at[here]))
        place += size

    @pl.loop(0, rows // chunk)
    def _(number):
        here = pl.ds(pl.multiple_of(number * chunk, chunk), chunk)
        gedges_ref[here, :] = (
            cot_v[here, :].astype(jnp.float32) + dot(gpre[here, :], weight(1), NT)
        ).astype(jnp.bfloat16)

    own = dot(oht[pl.ds(0, node_dev), :], gpre[...])
    received = dot(oht[pl.ds(2 * node_dev, node_dev), :], gpre[...])
    received = dot(received.astype(jnp.bfloat16), weight(3), NT) + ncot_v[...].astype(
        jnp.float32
    )
    for arrival in back_msgs:
        arrival.wait_recv()
    got = back_in[...].astype(jnp.float32)
    coarse = got[3 * rim : 3 * rim + COARSE] + got[3 * rim + COARSE :]
    low = own[:rim] + got[rim : 2 * rim]
    low = jnp.concatenate([low[:COARSE] + coarse, low[COARSE:]], axis=0)
    middle = own[rim : 2 * rim] + got[2 * rim : 3 * rim]
    high = own[node_dev - rim :] + got[:rim]
    own = jnp.concatenate([low, middle, own[2 * rim : node_dev - rim], high], axis=0)
    gnodes_ref[...] = (received + dot(own.astype(jnp.bfloat16), weight(2), NT)).astype(
        jnp.bfloat16
    )
    for copy in sent:
        copy.wait_send()


def write_out(edges_ref, nodes_ref, edges_hbm, nodes_hbm, sem):
    quarter = edges_ref.shape[0] // 4
    copies = [pltpu.make_async_copy(nodes_ref, nodes_hbm, sem.at[4])]
    for number in range(4):
        here = pl.ds(number * quarter, quarter)
        copies.append(
            pltpu.make_async_copy(edges_ref.at[here], edges_hbm.at[here], sem.at[number])
        )
    for copy in copies:
        copy.start()
    for copy in copies:
        copy.wait()


def per_device(
    n_bx,
    nodes,
    edges,
    edge_cotangent,
    node_cotangent,
    senders,
    receivers,
    slots,
    live,
    w_edge,
    w_send,
    w_recv,
    w_out,
    bias,
):
    shard_rows, width = w_edge.shape
    depth = shard_rows * n_bx
    gather = shard_rows % 64 == 0 and n_bx % 2 == 0
    weights = [w_out, w_edge, w_send, w_recv]
    if not gather:
        weights = [lax.all_gather(w, "bx", axis=0, tiled=True) for w in weights]
    nz = n_bx // 2
    rows = edges.shape[0]
    blocks = slots.shape[0]
    block = rows // blocks
    node_dev = nodes.shape[0]
    chunk = rows // 3
    cfg = (n_bx, gather, nz, shard_rows, chunk)
    bf16, f32 = jnp.bfloat16, jnp.float32
    wall = (4, nz, 2, shard_rows, width) if gather else (4, depth, width)
    count = 3 * nz + 64
    vmem = pl.BlockSpec(memory_space=pltpu.VMEM)
    hbm = pl.BlockSpec(memory_space=pl.ANY)
    results = pl.pallas_call(
        functools.partial(kernel, cfg),
        out_shape=(
            pltpu.VMEM((rows, width), bf16),
            pltpu.VMEM((node_dev, width), bf16),
        ),
        in_specs=[hbm] * 13,
        out_specs=(vmem, vmem),
        scratch_shapes=[
            pltpu.SMEM((blocks,), jnp.int32),
            pltpu.SMEM((blocks,), jnp.int32),
            pltpu.VMEM((blocks, block), jnp.int32),
            pltpu.VMEM((blocks, block), jnp.int32),
            pltpu.VMEM((1, width), f32),
            pltpu.VMEM(wall, bf16),
            pltpu.VMEM((2 * node_dev, width), bf16),
            pltpu.VMEM((rows, width), bf16),
            pltpu.VMEM((rows, width), bf16),
            pltpu.VMEM((node_dev, width), bf16),
            pltpu.VMEM((rows, 3 * node_dev), bf16),
            pltpu.VMEM((3 * node_dev, rows), bf16),
            pltpu.VMEM((rows, width), bf16),
            pltpu.VMEM((rows, width), f32),
            pltpu.VMEM((rows, width), f32),
            pltpu.VMEM((3 * node_dev, width), bf16),
            pltpu.VMEM((rows, width), bf16),
            pltpu.VMEM((node_dev, width), bf16),
            pltpu.VMEM((node_dev, width), bf16),
            pltpu.SemaphoreType.DMA((13,)),
            pltpu.SemaphoreType.DMA((count,)),
            pltpu.SemaphoreType.DMA((count,)),
        ],
        compiler_params=pltpu.CompilerParams(
            collective_id=0, has_side_effects=True, vmem_limit_bytes=60 * 1024 * 1024
        ),
    )(
        slots,
        live,
        senders.reshape(blocks, block),
        receivers.reshape(blocks, block),
        bias.reshape(1, width),
        nodes,
        edges,
        edge_cotangent,
        node_cotangent,
        *weights,
    )
    return pl.pallas_call(
        write_out,
        out_shape=(
            jax.ShapeDtypeStruct((rows, width), bf16),
            jax.ShapeDtypeStruct((node_dev, width), bf16),
        ),
        in_specs=[vmem, vmem],
        out_specs=(hbm, hbm),
        scratch_shapes=[pltpu.SemaphoreType.DMA((5,))],
        compiler_params=pltpu.CompilerParams(vmem_limit_bytes=1024 * 1024),
    )(*results)


def solution(mesh):
    n_bx = mesh.shape["bx"]
    in_specs = (
        P(("ens", "bx", "by"), None),
        P(("ens", "bx", "by"), None),
        P(("ens", "bx", "by"), None),
        P(("ens", "bx", "by"), None),
        P(("ens", "bx", "by")),
        P(("ens", "bx", "by")),
        P(("ens", "bx", "by")),
        P(("ens", "bx", "by")),
        P("bx", None),
        P("bx", None),
        P("bx", None),
        P("bx", None),
        P(),
    )
    out_specs = (P(("ens", "bx", "by"), None), P(("ens", "bx", "by"), None))
    return jax.shard_map(
        functools.partial(per_device, n_bx),
        mesh=mesh,
        in_specs=in_specs,
        out_specs=out_specs,
        check_vma=False,
    )
```

```python
import functools

import jax
import jax.numpy as jnp
from jax import lax
from jax.experimental import pallas as pl
from jax.experimental.pallas import tpu as pltpu
from jax.sharding import PartitionSpec as P

COARSE = 16
MESH = pl.DeviceIdType.MESH
NN = (((1,), (0,)), ((), ()))
NT = (((1,), (1,)), ((), ()))


def dot(a, b, dims=NN):
    return lax.dot_general(a, b, dims, preferred_element_type=jnp.float32)


def flip(index, apart):
    return index + apart * (1 - 2 * ((index // apart) % 2))


def kernel(
    cfg,
    slots_hbm,
    live_hbm,
    senders_hbm,
    receivers_hbm,
    bias_hbm,
    nodes_hbm,
    edges_hbm,
    cot_hbm,
    ncot_hbm,
    wout_hbm,
    wedge_hbm,
    wsend_hbm,
    wrecv_hbm,
    gedges_ref,
    gnodes_ref,
    slots_ref,
    live_ref,
    senders_ref,
    receivers_ref,
    bias_ref,
    wall,
    table,
    edges_v,
    cot_v,
    ncot_v,
    oh,
    oht,
    gmsg,
    gact,
    pre,
    proj,
    gpre,
    back_out,
    back_in,
    local_sem,
    send_sem,
    recv_sem,
):
    n_bx, gather, nz, shard_rows, chunk = cfg
    node_dev = ncot_v.shape[0]
    rim = node_dev // 4
    block = senders_ref.shape[1]
    blocks = senders_ref.shape[0]
    rows = edges_v.shape[0]
    ens, bx, by = lax.axis_index("ens"), lax.axis_index("bx"), lax.axis_index("by")
    z, x = bx // 2, bx % 2

    right = (ens, (bx + 1) % n_bx, by)
    left = (ens, (bx + n_bx - 1) % n_bx, by)
    core = (ens, bx, 1 - by)
    far = [(ens, flip(bx, n_bx // 2), by), (ens, flip(bx, n_bx // 4), by)]
    x_peer = (ens, z * 2 + 1 - x, by)
    y_peer = (1 - ens, bx, by)
    greeted = [right, left, core] + far
    if gather:
        greeted += [(ens, ((z + dz) % nz) * 2 + x, by) for dz in range(1, nz)]
        greeted += [x_peer, y_peer]

    barrier = pltpu.get_barrier_semaphore()
    for device in greeted:
        pl.semaphore_signal(barrier, inc=1, device_id=device, device_id_type=MESH)
    def local(source, target, number):
        return pltpu.make_async_copy(source, target, local_sem.at[number])

    weights = (wout_hbm, wedge_hbm, wsend_hbm, wrecv_hbm)
    w_copies = []
    for number, ref in enumerate(weights):
        target = wall.at[number, z, x] if gather else wall.at[number]
        w_copies.append(local(ref, target, number))
    nodes_copy = local(nodes_hbm, table.at[pl.ds(0, node_dev)], 4)
    ncot_copy = local(ncot_hbm, ncot_v, 5)
    cot_copy = local(cot_hbm, cot_v, 6)
    edges_copy = local(edges_hbm, edges_v, 7)
    small_copies = [
        local(slots_hbm, slots_ref, 8),
        local(live_hbm, live_ref, 9),
        local(senders_hbm, senders_ref, 10),
        local(receivers_hbm, receivers_ref, 11),
        local(bias_hbm, bias_ref, 12),
    ]
    for copy in w_copies + [nodes_copy] + small_copies + [ncot_copy, cot_copy, edges_copy]:
        copy.start()

    pl.semaphore_wait(barrier, len(greeted))

    used = [0]
    sent = []

    def message(source, target, device, incoming):
        number = used[0]
        used[0] += 1
        out = pltpu.make_async_remote_copy(
            src_ref=source,
            dst_ref=target,
            send_sem=send_sem.at[number],
            recv_sem=recv_sem.at[number],
            device_id=device,
            device_id_type=MESH,
        )
        out.start()
        sent.append(out)
        return pltpu.make_async_remote_copy(
            src_ref=incoming,
            dst_ref=incoming,
            send_sem=send_sem.at[number],
            recv_sem=recv_sem.at[number],
            device_id=device,
            device_id_type=MESH,
        )

    nodes_copy.wait()
    pieces = [
        (node_dev - rim, rim, right),
        (0, rim, left),
        (rim, rim, core),
        (0, COARSE, far[0]),
        (0, COARSE, far[1]),
    ]
    shared = 2

    def part_a(zz, xx, e, b):
        size = shard_rows // 4
        start = pl.multiple_of((2 * e + b) * size, size)
        return wall.at[pl.ds(0, shared), zz, xx, pl.ds(start, size)]

    def part_b(zz, xx, e, b):
        size = shard_rows // 2
        start = pl.multiple_of(b * size, size)
        return wall.at[pl.ds(shared, 4 - shared), zz, xx, pl.ds(start, size)]

    def other(step):
        out = z
        if step & 1:
            out = flip(out, 1)
        if step & 2:
            out = flip(out, 2)
        return out

    def z_sends(part):
        got = []
        own = part(z, x, ens, by)
        for dz in range(1, nz):
            incoming = part(other(dz), x, ens, by)
            got.append(message(own, own, (ens, other(dz) * 2 + x, by), incoming))
        return got

    def forward(part, dz, xx, e, b, device, arrives):
        zz = other(dz)
        source = part(zz, xx, e, b)
        return message(source, source, device, part(zz, *arrives))

    def to_x(part, dz):
        return forward(part, dz, x, ens, by, x_peer, (1 - x, ens, by))

    def to_y(part, dz, xx):
        return forward(part, dz, xx, ens, by, y_peer, (xx, 1 - ens, by))

    def to_core(part, dz, xx, e):
        return forward(part, dz, xx, e, by, core, (xx, e, 1 - by))

    def prepare(first, last):
        @pl.loop(first, last)
        def _(number):
            row = pl.multiple_of(number * block, block)
            here = pl.ds(row, block)
            slot = slots_ref[number]
            offset = jnp.where(slot == 0, 0, node_dev)
            offset = offset + jnp.where(slot == 2, rim, 0)
            offset = offset + jnp.where(slot == 3, 2 * rim, 0)
            offset = offset + jnp.where(slot >= 4, 3 * rim, 0)
            offset = offset + jnp.where(slot == 5, COARSE, 0)
            sender = senders_ref[pl.ds(number, 1), :] + offset
            receiver = receivers_ref[pl.ds(number, 1), :]
            lines = lax.broadcasted_iota(jnp.int32, (2 * node_dev, block), 0)
            hot_s = jnp.where(lines == sender, 1.0, 0.0)
            lines = lax.broadcasted_iota(jnp.int32, (node_dev, block), 0)
            hot_r = jnp.where(lines == receiver, 1.0, 0.0)
            hot = jnp.concatenate([hot_s, hot_r], axis=0)
            oht[:, here] = hot.astype(jnp.bfloat16)
            turned = hot.T.astype(jnp.bfloat16)
            oh[here, :] = turned
            ncot = dot(turned[:, 2 * node_dev :], ncot_v[...])
            total = cot_v[here, :].astype(jnp.float32) + ncot
            lines = lax.broadcasted_iota(jnp.int32, total.shape, 0)
            total = jnp.where(lines < live_ref[number], total, 0.0)
            gmsg[here, :] = total.astype(jnp.bfloat16)

    third = blocks // 3
    for copy in w_copies:
        copy.wait()
    if gather:
        a_z = z_sends(part_a)
        a_x = [to_x(part_a, 0)]
        b_z = z_sends(part_b)
        b_x = [to_x(part_b, 0)]
    node_msgs = []
    place = node_dev
    for start, size, device in pieces:
        target = table.at[pl.ds(place, size)]
        node_msgs.append(message(table.at[pl.ds(start, size)], target, device, target))
        place += size
    for copy in small_copies + [ncot_copy, cot_copy]:
        copy.wait()
    prepare(0, third)
    a_y, a_c, a_c2, b_c = [], [], [], []
    if gather:
        for dz in range(1, nz):
            a_z[dz - 1].wait_recv()
            a_x.append(to_x(part_a, dz))
            a_y.append((dz, x, to_y(part_a, dz, x)))
            a_c.append(to_core(part_a, dz, x, ens))
        prepare(third, 2 * third)
        for dz in range(nz):
            a_x[dz].wait_recv()
            a_y.append((dz, 1 - x, to_y(part_a, dz, 1 - x)))
            a_c.append(to_core(part_a, dz, 1 - x, ens))
            if dz:
                b_z[dz - 1].wait_recv()
                b_x.append(to_x(part_b, dz))
                b_c.append(to_core(part_b, dz, x, ens))
        prepare(2 * third, blocks)
        for dz, xx, arrival in a_y[: nz - 1]:
            arrival.wait_recv()
            a_c2.append(to_core(part_a, dz, xx, 1 - ens))
        for dz, xx, arrival in a_y[nz - 1 :]:
            arrival.wait_recv()
            a_c2.append(to_core(part_a, dz, xx, 1 - ens))
            b_x[dz].wait_recv()
            b_c.append(to_core(part_b, dz, 1 - x, ens))
        for arrival in a_c + a_c2:
            arrival.wait_recv()
    else:
        prepare(third, blocks)

    def weight(number):
        value = wall[number]
        return value.reshape(-1, value.shape[-1])

    edges_copy.wait()

    for arrival in b_c + node_msgs:
        arrival.wait_recv()
    proj[pl.ds(0, 2 * node_dev), :] = dot(table[...], weight(2)).astype(jnp.bfloat16)
    proj[pl.ds(2 * node_dev, node_dev), :] = dot(
        table[pl.ds(0, node_dev), :], weight(3)
    ).astype(jnp.bfloat16)

    for number in range(rows // chunk):
        here = pl.ds(number * chunk, chunk)
        act = dot(edges_v[here, :], weight(1)) + dot(oh[here, :], proj[...]) + bias_ref[...]
        sigma = 0.5 + 0.5 * jnp.tanh(0.5 * act)
        slope = sigma * (1.0 + act * (1.0 - sigma))
        gpre[here, :] = (dot(gmsg[here, :], weight(0), NT) * slope).astype(jnp.bfloat16)

    back_out[...] = dot(oht[pl.ds(node_dev, node_dev), :], gpre[...]).astype(jnp.bfloat16)
    backs = [(rim, left), (rim, right), (rim, core), (COARSE, far[0]), (COARSE, far[1])]
    back_msgs = []
    place = 0
    for size, device in backs:
        here = pl.ds(place, size)
        back_msgs.append(message(back_out.at[here], back_in.at[here], device, back_in.at[here]))
        place += size

    @pl.loop(0, rows // chunk)
    def _(number):
        here = pl.ds(pl.multiple_of(number * chunk, chunk), chunk)
        gedges_ref[here, :] = (
            cot_v[here, :].astype(jnp.float32) + dot(gpre[here, :], weight(1), NT)
        ).astype(jnp.bfloat16)

    own = dot(oht[pl.ds(0, node_dev), :], gpre[...])
    received = dot(oht[pl.ds(2 * node_dev, node_dev), :], gpre[...])
    received = dot(received.astype(jnp.bfloat16), weight(3), NT) + ncot_v[...].astype(
        jnp.float32
    )
    for copy in sent:
        copy.wait_send()
    for arrival in back_msgs:
        arrival.wait_recv()
    got = back_in[...].astype(jnp.float32)
    coarse = got[3 * rim : 3 * rim + COARSE] + got[3 * rim + COARSE :]
    low = own[:rim] + got[rim : 2 * rim]
    low = jnp.concatenate([low[:COARSE] + coarse, low[COARSE:]], axis=0)
    middle = own[rim : 2 * rim] + got[2 * rim : 3 * rim]
    high = own[node_dev - rim :] + got[:rim]
    own = jnp.concatenate([low, middle, own[2 * rim : node_dev - rim], high], axis=0)
    gnodes_ref[...] = (received + dot(own.astype(jnp.bfloat16), weight(2), NT)).astype(
        jnp.bfloat16
    )


def write_out(edges_ref, nodes_ref, edges_hbm, nodes_hbm, sem):
    quarter = edges_ref.shape[0] // 4
    copies = [pltpu.make_async_copy(nodes_ref, nodes_hbm, sem.at[4])]
    for number in range(4):
        here = pl.ds(number * quarter, quarter)
        copies.append(
            pltpu.make_async_copy(edges_ref.at[here], edges_hbm.at[here], sem.at[number])
        )
    for copy in copies:
        copy.start()
    for copy in copies:
        copy.wait()


def per_device(
    n_bx,
    nodes,
    edges,
    edge_cotangent,
    node_cotangent,
    senders,
    receivers,
    slots,
    live,
    w_edge,
    w_send,
    w_recv,
    w_out,
    bias,
):
    shard_rows, width = w_edge.shape
    depth = shard_rows * n_bx
    gather = shard_rows % 64 == 0 and n_bx % 2 == 0
    weights = [w_out, w_edge, w_send, w_recv]
    if not gather:
        weights = [lax.all_gather(w, "bx", axis=0, tiled=True) for w in weights]
    nz = n_bx // 2
    rows = edges.shape[0]
    blocks = slots.shape[0]
    block = rows // blocks
    node_dev = nodes.shape[0]
    chunk = rows // 3
    cfg = (n_bx, gather, nz, shard_rows, chunk)
    bf16, f32 = jnp.bfloat16, jnp.float32
    wall = (4, nz, 2, shard_rows, width) if gather else (4, depth, width)
    count = 3 * nz + 64
    vmem = pl.BlockSpec(memory_space=pltpu.VMEM)
    hbm = pl.BlockSpec(memory_space=pl.ANY)
    results = pl.pallas_call(
        functools.partial(kernel, cfg),
        out_shape=(
            pltpu.VMEM((rows, width), bf16),
            pltpu.VMEM((node_dev, width), bf16),
        ),
        in_specs=[hbm] * 13,
        out_specs=(vmem, vmem),
        scratch_shapes=[
            pltpu.SMEM((blocks,), jnp.int32),
            pltpu.SMEM((blocks,), jnp.int32),
            pltpu.VMEM((blocks, block), jnp.int32),
            pltpu.VMEM((blocks, block), jnp.int32),
            pltpu.VMEM((1, width), f32),
            pltpu.VMEM(wall, bf16),
            pltpu.VMEM((2 * node_dev, width), bf16),
            pltpu.VMEM((rows, width), bf16),
            pltpu.VMEM((rows, width), bf16),
            pltpu.VMEM((node_dev, width), bf16),
            pltpu.VMEM((rows, 3 * node_dev), bf16),
            pltpu.VMEM((3 * node_dev, rows), bf16),
            pltpu.VMEM((rows, width), bf16),
            pltpu.VMEM((rows, width), f32),
            pltpu.VMEM((rows, width), f32),
            pltpu.VMEM((3 * node_dev, width), bf16),
            pltpu.VMEM((rows, width), bf16),
            pltpu.VMEM((node_dev, width), bf16),
            pltpu.VMEM((node_dev, width), bf16),
            pltpu.SemaphoreType.DMA((13,)),
            pltpu.SemaphoreType.DMA((count,)),
            pltpu.SemaphoreType.DMA((count,)),
        ],
        compiler_params=pltpu.CompilerParams(
            collective_id=0, has_side_effects=True, vmem_limit_bytes=60 * 1024 * 1024
        ),
    )(
        slots,
        live,
        senders.reshape(blocks, block),
        receivers.reshape(blocks, block),
        bias.reshape(1, width),
        nodes,
        edges,
        edge_cotangent,
        node_cotangent,
        *weights,
    )
    return pl.pallas_call(
        write_out,
        out_shape=(
            jax.ShapeDtypeStruct((rows, width), bf16),
            jax.ShapeDtypeStruct((node_dev, width), bf16),
        ),
        in_specs=[vmem, vmem],
        out_specs=(hbm, hbm),
        scratch_shapes=[pltpu.SemaphoreType.DMA((5,))],
        compiler_params=pltpu.CompilerParams(vmem_limit_bytes=1024 * 1024),
    )(*results)


def solution(mesh):
    n_bx = mesh.shape["bx"]
    in_specs = (
        P(("ens", "bx", "by"), None),
        P(("ens", "bx", "by"), None),
        P(("ens", "bx", "by"), None),
        P(("ens", "bx", "by"), None),
        P(("ens", "bx", "by")),
        P(("ens", "bx", "by")),
        P(("ens", "bx", "by")),
        P(("ens", "bx", "by")),
        P("bx", None),
        P("bx", None),
        P("bx", None),
        P("bx", None),
        P(),
    )
    out_specs = (P(("ens", "bx", "by"), None), P(("ens", "bx", "by"), None))
    return jax.shard_map(
        functools.partial(per_device, n_bx),
        mesh=mesh,
        in_specs=in_specs,
        out_specs=out_specs,
        check_vma=False,
    )
```

```python
import functools

import jax
import jax.numpy as jnp
from jax import lax
from jax.experimental import pallas as pl
from jax.experimental.pallas import tpu as pltpu
from jax.sharding import PartitionSpec as P

COARSE = 16
MESH = pl.DeviceIdType.MESH
NN = (((1,), (0,)), ((), ()))
NT = (((1,), (1,)), ((), ()))


def dot(a, b, dims=NN):
    return lax.dot_general(a, b, dims, preferred_element_type=jnp.float32)


def flip(index, apart):
    return index + apart * (1 - 2 * ((index // apart) % 2))


def kernel(
    cfg,
    slots_hbm,
    live_hbm,
    senders_hbm,
    receivers_hbm,
    bias_hbm,
    nodes_hbm,
    edges_hbm,
    cot_hbm,
    ncot_hbm,
    wout_hbm,
    wedge_hbm,
    wsend_hbm,
    wrecv_hbm,
    gedges_ref,
    gnodes_ref,
    slots_ref,
    live_ref,
    senders_ref,
    receivers_ref,
    bias_ref,
    wall,
    table,
    edges_v,
    cot_v,
    ncot_v,
    oh,
    oht,
    gmsg,
    gact,
    pre,
    proj,
    gpre,
    back_out,
    back_in,
    local_sem,
    send_sem,
    recv_sem,
):
    n_bx, gather, nz, shard_rows, chunk = cfg
    node_dev = ncot_v.shape[0]
    rim = node_dev // 4
    block = senders_ref.shape[1]
    blocks = senders_ref.shape[0]
    rows = edges_v.shape[0]
    ens, bx, by = lax.axis_index("ens"), lax.axis_index("bx"), lax.axis_index("by")
    z, x = bx // 2, bx % 2

    right = (ens, (bx + 1) % n_bx, by)
    left = (ens, (bx + n_bx - 1) % n_bx, by)
    core = (ens, bx, 1 - by)
    far = [(ens, flip(bx, n_bx // 2), by), (ens, flip(bx, n_bx // 4), by)]
    x_peer = (ens, z * 2 + 1 - x, by)
    y_peer = (1 - ens, bx, by)
    greeted = [right, left, core] + far
    if gather:
        greeted += [(ens, ((z + dz) % nz) * 2 + x, by) for dz in range(1, nz)]
        greeted += [x_peer, y_peer]

    barrier = pltpu.get_barrier_semaphore()
    for device in greeted:
        pl.semaphore_signal(barrier, inc=1, device_id=device, device_id_type=MESH)
    def local(source, target, number):
        return pltpu.make_async_copy(source, target, local_sem.at[number])

    weights = (wout_hbm, wedge_hbm, wsend_hbm, wrecv_hbm)
    w_copies = []
    for number, ref in enumerate(weights):
        target = wall.at[number, z, x] if gather else wall.at[number]
        w_copies.append(local(ref, target, number))
    nodes_copy = local(nodes_hbm, table.at[pl.ds(0, node_dev)], 4)
    ncot_copy = local(ncot_hbm, ncot_v, 5)
    cot_copy = local(cot_hbm, cot_v, 6)
    edges_copy = local(edges_hbm, edges_v, 7)
    small_copies = [
        local(slots_hbm, slots_ref, 8),
        local(live_hbm, live_ref, 9),
        local(senders_hbm, senders_ref, 10),
        local(receivers_hbm, receivers_ref, 11),
        local(bias_hbm, bias_ref, 12),
    ]
    for copy in w_copies + [nodes_copy] + small_copies + [ncot_copy, cot_copy, edges_copy]:
        copy.start()

    pl.semaphore_wait(barrier, len(greeted))

    used = [0]
    sent = []

    def message(source, target, device, incoming):
        number = used[0]
        used[0] += 1
        out = pltpu.make_async_remote_copy(
            src_ref=source,
            dst_ref=target,
            send_sem=send_sem.at[number],
            recv_sem=recv_sem.at[number],
            device_id=device,
            device_id_type=MESH,
        )
        out.start()
        sent.append(out)
        return pltpu.make_async_remote_copy(
            src_ref=incoming,
            dst_ref=incoming,
            send_sem=send_sem.at[number],
            recv_sem=recv_sem.at[number],
            device_id=device,
            device_id_type=MESH,
        )

    nodes_copy.wait()
    pieces = [
        (node_dev - rim, rim, right),
        (0, rim, left),
        (rim, rim, core),
        (0, COARSE, far[0]),
        (0, COARSE, far[1]),
    ]
    shared = 2

    def part_a(zz, xx, e, b):
        size = shard_rows // 4
        start = pl.multiple_of((2 * e + b) * size, size)
        return wall.at[pl.ds(0, shared), zz, xx, pl.ds(start, size)]

    def part_b(zz, xx, e, b):
        size = shard_rows // 2
        start = pl.multiple_of(b * size, size)
        return wall.at[pl.ds(shared, 4 - shared), zz, xx, pl.ds(start, size)]

    def other(step):
        out = z
        if step & 1:
            out = flip(out, 1)
        if step & 2:
            out = flip(out, 2)
        return out

    def z_sends(part):
        got = []
        own = part(z, x, ens, by)
        for dz in range(1, nz):
            incoming = part(other(dz), x, ens, by)
            got.append(message(own, own, (ens, other(dz) * 2 + x, by), incoming))
        return got

    def forward(part, dz, xx, e, b, device, arrives):
        zz = other(dz)
        source = part(zz, xx, e, b)
        return message(source, source, device, part(zz, *arrives))

    def to_x(part, dz):
        return forward(part, dz, x, ens, by, x_peer, (1 - x, ens, by))

    def to_y(part, dz, xx):
        return forward(part, dz, xx, ens, by, y_peer, (xx, 1 - ens, by))

    def to_core(part, dz, xx, e):
        return forward(part, dz, xx, e, by, core, (xx, e, 1 - by))

    def column_to_core(xx, e):
        size = shard_rows // 4

        def column(b):
            start = pl.multiple_of((2 * e + b) * size, size)
            return wall.at[pl.ds(0, shared), :, xx, pl.ds(start, size)]

        return message(column(by), column(by), core, column(1 - by))

    def prepare(first, last):
        @pl.loop(first, last)
        def _(number):
            row = pl.multiple_of(number * block, block)
            here = pl.ds(row, block)
            slot = slots_ref[number]
            offset = jnp.where(slot == 0, 0, node_dev)
            offset = offset + jnp.where(slot == 2, rim, 0)
            offset = offset + jnp.where(slot == 3, 2 * rim, 0)
            offset = offset + jnp.where(slot >= 4, 3 * rim, 0)
            offset = offset + jnp.where(slot == 5, COARSE, 0)
            sender = senders_ref[pl.ds(number, 1), :] + offset
            receiver = receivers_ref[pl.ds(number, 1), :]
            lines = lax.broadcasted_iota(jnp.int32, (2 * node_dev, block), 0)
            hot_s = jnp.where(lines == sender, 1.0, 0.0)
            lines = lax.broadcasted_iota(jnp.int32, (node_dev, block), 0)
            hot_r = jnp.where(lines == receiver, 1.0, 0.0)
            hot = jnp.concatenate([hot_s, hot_r], axis=0)
            oht[:, here] = hot.astype(jnp.bfloat16)
            turned = hot.T.astype(jnp.bfloat16)
            oh[here, :] = turned
            ncot = dot(turned[:, 2 * node_dev :], ncot_v[...])
            total = cot_v[here, :].astype(jnp.float32) + ncot
            lines = lax.broadcasted_iota(jnp.int32, total.shape, 0)
            total = jnp.where(lines < live_ref[number], total, 0.0)
            gmsg[here, :] = total.astype(jnp.bfloat16)

    third = blocks // 3
    for copy in w_copies:
        copy.wait()
    if gather:
        a_z = z_sends(part_a)
        a_x = [to_x(part_a, 0)]
        b_z = z_sends(part_b)
        b_x = [to_x(part_b, 0)]
    node_msgs = []
    place = node_dev
    for start, size, device in pieces:
        target = table.at[pl.ds(place, size)]
        node_msgs.append(message(table.at[pl.ds(start, size)], target, device, target))
        place += size
    for copy in small_copies + [ncot_copy, cot_copy]:
        copy.wait()
    prepare(0, third)
    a_y, a_c, a_c2, b_c = [], [], [], []
    if gather:
        for dz in range(1, nz):
            a_z[dz - 1].wait_recv()
            a_x.append(to_x(part_a, dz))
            a_y.append((dz, x, to_y(part_a, dz, x)))
            a_c.append(to_core(part_a, dz, x, ens))
        prepare(third, 2 * third)
        for dz in range(nz):
            a_x[dz].wait_recv()
            a_y.append((dz, 1 - x, to_y(part_a, dz, 1 - x)))
        a_c.append(column_to_core(1 - x, ens))
        for dz in range(1, nz):
            b_z[dz - 1].wait_recv()
            b_x.append(to_x(part_b, dz))
            b_c.append(to_core(part_b, dz, x, ens))
        prepare(2 * third, blocks)
        for dz, xx, arrival in a_y:
            arrival.wait_recv()
            if dz and xx is x:
                a_c2.append(to_core(part_a, dz, xx, 1 - ens))
        a_c2.append(column_to_core(1 - x, 1 - ens))
        for dz in range(nz):
            b_x[dz].wait_recv()
            b_c.append(to_core(part_b, dz, 1 - x, ens))
        for arrival in a_c + a_c2:
            arrival.wait_recv()
    else:
        prepare(third, blocks)

    def weight(number):
        value = wall[number]
        return value.reshape(-1, value.shape[-1])

    edges_copy.wait()

    for arrival in b_c + node_msgs:
        arrival.wait_recv()
    proj[pl.ds(0, 2 * node_dev), :] = dot(table[...], weight(2)).astype(jnp.bfloat16)
    proj[pl.ds(2 * node_dev, node_dev), :] = dot(
        table[pl.ds(0, node_dev), :], weight(3)
    ).astype(jnp.bfloat16)

    for number in range(rows // chunk):
        here = pl.ds(number * chunk, chunk)
        act = dot(edges_v[here, :], weight(1)) + dot(oh[here, :], proj[...]) + bias_ref[...]
        sigma = 0.5 + 0.5 * jnp.tanh(0.5 * act)
        slope = sigma * (1.0 + act * (1.0 - sigma))
        gpre[here, :] = (dot(gmsg[here, :], weight(0), NT) * slope).astype(jnp.bfloat16)

    back_out[...] = dot(oht[pl.ds(node_dev, node_dev), :], gpre[...]).astype(jnp.bfloat16)
    backs = [(rim, left), (rim, right), (rim, core), (COARSE, far[0]), (COARSE, far[1])]
    back_msgs = []
    place = 0
    for size, device in backs:
        here = pl.ds(place, size)
        back_msgs.append(message(back_out.at[here], back_in.at[here], device, back_in.at[here]))
        place += size

    @pl.loop(0, rows // chunk)
    def _(number):
        here = pl.ds(pl.multiple_of(number * chunk, chunk), chunk)
        gedges_ref[here, :] = (
            cot_v[here, :].astype(jnp.float32) + dot(gpre[here, :], weight(1), NT)
        ).astype(jnp.bfloat16)

    own = dot(oht[pl.ds(0, node_dev), :], gpre[...])
    received = dot(oht[pl.ds(2 * node_dev, node_dev), :], gpre[...])
    received = dot(received.astype(jnp.bfloat16), weight(3), NT) + ncot_v[...].astype(
        jnp.float32
    )
    for copy in sent:
        copy.wait_send()
    for arrival in back_msgs:
        arrival.wait_recv()
    got = back_in[...].astype(jnp.float32)
    coarse = got[3 * rim : 3 * rim + COARSE] + got[3 * rim + COARSE :]
    low = own[:rim] + got[rim : 2 * rim]
    low = jnp.concatenate([low[:COARSE] + coarse, low[COARSE:]], axis=0)
    middle = own[rim : 2 * rim] + got[2 * rim : 3 * rim]
    high = own[node_dev - rim :] + got[:rim]
    own = jnp.concatenate([low, middle, own[2 * rim : node_dev - rim], high], axis=0)
    gnodes_ref[...] = (received + dot(own.astype(jnp.bfloat16), weight(2), NT)).astype(
        jnp.bfloat16
    )


def write_out(edges_ref, nodes_ref, edges_hbm, nodes_hbm, sem):
    quarter = edges_ref.shape[0] // 4
    copies = [pltpu.make_async_copy(nodes_ref, nodes_hbm, sem.at[4])]
    for number in range(4):
        here = pl.ds(number * quarter, quarter)
        copies.append(
            pltpu.make_async_copy(edges_ref.at[here], edges_hbm.at[here], sem.at[number])
        )
    for copy in copies:
        copy.start()
    for copy in copies:
        copy.wait()


def per_device(
    n_bx,
    nodes,
    edges,
    edge_cotangent,
    node_cotangent,
    senders,
    receivers,
    slots,
    live,
    w_edge,
    w_send,
    w_recv,
    w_out,
    bias,
):
    shard_rows, width = w_edge.shape
    depth = shard_rows * n_bx
    gather = shard_rows % 64 == 0 and n_bx % 2 == 0
    weights = [w_out, w_edge, w_send, w_recv]
    if not gather:
        weights = [lax.all_gather(w, "bx", axis=0, tiled=True) for w in weights]
    nz = n_bx // 2
    rows = edges.shape[0]
    blocks = slots.shape[0]
    block = rows // blocks
    node_dev = nodes.shape[0]
    chunk = rows // 3
    cfg = (n_bx, gather, nz, shard_rows, chunk)
    bf16, f32 = jnp.bfloat16, jnp.float32
    wall = (4, nz, 2, shard_rows, width) if gather else (4, depth, width)
    count = 3 * nz + 64
    vmem = pl.BlockSpec(memory_space=pltpu.VMEM)
    hbm = pl.BlockSpec(memory_space=pl.ANY)
    results = pl.pallas_call(
        functools.partial(kernel, cfg),
        out_shape=(
            pltpu.VMEM((rows, width), bf16),
            pltpu.VMEM((node_dev, width), bf16),
        ),
        in_specs=[hbm] * 13,
        out_specs=(vmem, vmem),
        scratch_shapes=[
            pltpu.SMEM((blocks,), jnp.int32),
            pltpu.SMEM((blocks,), jnp.int32),
            pltpu.VMEM((blocks, block), jnp.int32),
            pltpu.VMEM((blocks, block), jnp.int32),
            pltpu.VMEM((1, width), f32),
            pltpu.VMEM(wall, bf16),
            pltpu.VMEM((2 * node_dev, width), bf16),
            pltpu.VMEM((rows, width), bf16),
            pltpu.VMEM((rows, width), bf16),
            pltpu.VMEM((node_dev, width), bf16),
            pltpu.VMEM((rows, 3 * node_dev), bf16),
            pltpu.VMEM((3 * node_dev, rows), bf16),
            pltpu.VMEM((rows, width), bf16),
            pltpu.VMEM((rows, width), f32),
            pltpu.VMEM((rows, width), f32),
            pltpu.VMEM((3 * node_dev, width), bf16),
            pltpu.VMEM((rows, width), bf16),
            pltpu.VMEM((node_dev, width), bf16),
            pltpu.VMEM((node_dev, width), bf16),
            pltpu.SemaphoreType.DMA((13,)),
            pltpu.SemaphoreType.DMA((count,)),
            pltpu.SemaphoreType.DMA((count,)),
        ],
        compiler_params=pltpu.CompilerParams(
            collective_id=0, has_side_effects=True, vmem_limit_bytes=60 * 1024 * 1024
        ),
    )(
        slots,
        live,
        senders.reshape(blocks, block),
        receivers.reshape(blocks, block),
        bias.reshape(1, width),
        nodes,
        edges,
        edge_cotangent,
        node_cotangent,
        *weights,
    )
    return pl.pallas_call(
        write_out,
        out_shape=(
            jax.ShapeDtypeStruct((rows, width), bf16),
            jax.ShapeDtypeStruct((node_dev, width), bf16),
        ),
        in_specs=[vmem, vmem],
        out_specs=(hbm, hbm),
        scratch_shapes=[pltpu.SemaphoreType.DMA((5,))],
        compiler_params=pltpu.CompilerParams(vmem_limit_bytes=1024 * 1024),
    )(*results)


def solution(mesh):
    n_bx = mesh.shape["bx"]
    in_specs = (
        P(("ens", "bx", "by"), None),
        P(("ens", "bx", "by"), None),
        P(("ens", "bx", "by"), None),
        P(("ens", "bx", "by"), None),
        P(("ens", "bx", "by")),
        P(("ens", "bx", "by")),
        P(("ens", "bx", "by")),
        P(("ens", "bx", "by")),
        P("bx", None),
        P("bx", None),
        P("bx", None),
        P("bx", None),
        P(),
    )
    out_specs = (P(("ens", "bx", "by"), None), P(("ens", "bx", "by"), None))
    return jax.shard_map(
        functools.partial(per_device, n_bx),
        mesh=mesh,
        in_specs=in_specs,
        out_specs=out_specs,
        check_vma=False,
    )
```
